256 devices in a mesh: dp: 16 (over z, core), group: 16 (over x, y).
Axes of the slice: x: 4, y: 4, z: 8, core: 2. Of those that a mesh axis runs over, the one named last changes fastest.
Arguments:
- queries: bfloat16 [16, 16, 256, 1024], P('dp', 'group'), may hold values from -36 to 36
- resp_kv: bfloat16 [16, 16, 256, 256], P('dp', 'group'), may hold values from -4 to 4
- out_grad: bfloat16 [16, 16, 256, 1024], P('dp', 'group'), may hold values from -6 to 6
- prompt_key_value: bfloat16 [16, 2048, 256], P('dp', 'group'), may hold values from -12 to 12
- lengths: int32 [16, 16], P('dp', 'group'), may hold values from 1 to 256, 3072 in all within a row
- group_mask: int32 [16], P('dp'), may hold values from 0 to 1, as said below
Outputs:
- q_grad: bfloat16 [16, 16, 256, 1024], P('dp', 'group')
- response_key_value_gradient: bfloat16 [16, 16, 256, 256], P('dp', 'group')
- prompt_kv_grad: bfloat16 [16, 2048, 256], P('dp', 'group')
The draws below stay inside these ranges and needn't reach their ends.
Inputs may be any that keep to these rules, and one draw needn't show every extreme that they name: The 16 lengths of each group sum to 3072, and the longest response of each group has exactly 256 tokens. `group_mask`: at least one group survives.
All inputs are finite; a program needn't handle non-finite values.
Results may differ from the reference program's by a relative error of at most 0.025.
Values may be sent and summed in bfloat16 or wider, within the bound.
A program may use at most 128 MiB of HBM per device.

```python
import math
import jax
import jax.numpy as jnp
import numpy as np
from jax import lax

HEAD = 128
QHEADS = 8
RESP = 256
PROMPT = 2048
PROMPT_GROUPS = 16
MEMBERS = 16
LTOT = 3072


def draw_prompt_key_value(key, part):
    key = jax.random.fold_in(key, 11)
    base = jnp.clip(jax.random.normal(key, (PROMPT_GROUPS, PROMPT, 2 * HEAD), jnp.float32), -4.0, 4.0)
    return base.astype(jnp.bfloat16)


def draw_queries(key, part):
    key = jax.random.fold_in(key, 12)
    base = jnp.clip(jax.random.normal(jax.random.fold_in(key, 1), (PROMPT_GROUPS, MEMBERS, RESP, QHEADS * HEAD), jnp.float32), -4.0, 4.0)
    return base.astype(jnp.bfloat16)


def draw_group_mask(key, part):
    key = jax.random.fold_in(key, 13)
    random_bernoulli = jax.random.randint(jax.random.fold_in(key, 1), (PROMPT_GROUPS,), 0, 2)
    living_group = jax.random.randint(jax.random.fold_in(key, 2), (), 0, PROMPT_GROUPS)
    return jnp.maximum(random_bernoulli, (jnp.arange(PROMPT_GROUPS) == living_group).astype(jnp.int32))


def levels(key, extent, cuts, smallest, largest):
    loudness = 1.0
    for dim, parts in cuts:
        draws = jax.random.uniform(jax.random.fold_in(jax.random.fold_in(key, 6), dim), (parts,), jnp.float32, smallest / len(cuts), largest / len(cuts))
        loudness = loudness * jnp.repeat(jnp.exp(draws), extent[dim] // parts).reshape((-1,) + (1,) * (len(extent) - 1 - dim))
    return loudness


def profile(count, total, most, skew):
    portions = [(1 << 20) // math.isqrt(rank ** skew) + 1 for rank in range(2, count + 1)]
    spare, counts = total - most - (count - 1), [1] * (count - 1)
    while spare > 0:
        free = [i for i in range(count - 1) if counts[i] < most]
        whole, left = sum([portions[i] for i in free]), spare
        for i in free:
            extra = min(most - counts[i], max(1, left * portions[i] // whole), spare)
            counts[i] = counts[i] + extra
            spare = spare - extra
    return np.array([most] + counts)


def uneven(rng, amount, total, most, skew):
    if amount == 2:
        one = jax.random.randint(rng, (), max(1, total - most), min(most, total - 1) + 1)
        return jnp.stack([one, total - one])
    sizes = jnp.asarray(profile(amount, total, most, skew), jnp.int32)
    pairs = (amount - 1) // 2
    source_of, receiver = sizes[1:1 + 2 * pairs:2], sizes[2:2 + 2 * pairs:2]
    margin = jnp.minimum(source_of - 1, most - receiver)
    shifted = jax.random.randint(jax.random.fold_in(rng, 1), (pairs,), 0, 1 << 20) % (margin + 1)
    sizes = sizes.at[1:1 + 2 * pairs:2].set(source_of - shifted).at[2:2 + 2 * pairs:2].set(receiver + shifted)
    return sizes[jax.random.permutation(jax.random.fold_in(rng, 2), amount)]


def gaussian(own_key, extent, spread, bound, shards=(), kind=jnp.bfloat16):
    values = jax.random.normal(own_key, extent, jnp.float32) * spread
    if len(shards) > 0:
        values = levels(own_key, extent, shards, -0.22, 0.18) * values
    return jnp.clip(values, min=-bound, max=bound).astype(kind)


def setup_inputs(seed: int = 0) -> dict:
    splits = jax.random.split(jax.random.key(seed), 7)
    return {
        "queries": draw_queries(jax.random.fold_in(splits[6], 71), 0),
        "resp_kv": gaussian(splits[1], (PROMPT_GROUPS, MEMBERS, RESP, 2 * HEAD), 1.0, 4.0, ((0, 16), (1, 16))),
        "out_grad": gaussian(splits[2], (PROMPT_GROUPS, MEMBERS, RESP, QHEADS * HEAD), 1.0, 6.0, ((0, 16), (1, 16))),
        "prompt_key_value": draw_prompt_key_value(jax.random.fold_in(splits[6], 71), 0),
        "lengths": jax.vmap(lambda own: uneven(own, MEMBERS, LTOT, RESP, 0))(jax.random.split(splits[4], PROMPT_GROUPS)).reshape((PROMPT_GROUPS, MEMBERS)).astype(jnp.int32),
        "group_mask": draw_group_mask(jax.random.fold_in(splits[6], 71), 0),
    }


def rounded(values_in):
    return lax.optimization_barrier(values_in.astype(jnp.bfloat16)).astype(jnp.float32)


def member_grads(query_rows, response_key_value, grad_in, prompt_keys, prompt_values, factor):
    inv_root = 1.0 / (HEAD ** 0.5)
    all_keys = jnp.concatenate([prompt_keys, response_key_value[:, :HEAD]], 0)
    all_values = jnp.concatenate([prompt_values, response_key_value[:, HEAD:]], 0)
    query_f32 = query_rows.reshape(RESP, QHEADS, HEAD).astype(jnp.float32)
    grad_f32 = grad_in.reshape(RESP, QHEADS, HEAD).astype(jnp.float32)
    keys_f32 = all_keys.astype(jnp.float32)
    values_f32 = all_values.astype(jnp.float32)
    scores = jnp.einsum('rhd,kd->hrk', query_f32, keys_f32) * inv_root
    column = jnp.arange(PROMPT + RESP)[None, :]
    row_index = jnp.arange(RESP)[:, None]
    allowed = (column < PROMPT) | (column - PROMPT <= row_index)
    scores = jnp.where(allowed[None], scores, -jnp.inf)
    highest = jnp.max(scores, -1, keepdims=True)
    log_total = highest + jnp.log(jnp.sum(jnp.exp(scores - highest), -1, keepdims=True))
    attn_probs = jnp.exp(scores - log_total)
    probs_low = rounded(attn_probs)
    attended = jnp.einsum('hrk,kd->hrd', probs_low, values_f32)
    row_dots = jnp.sum(jnp.transpose(grad_f32, (1, 0, 2)) * attended, -1, keepdims=True)
    dprobs = jnp.einsum('rhd,kd->hrk', grad_f32, values_f32)
    dscores = rounded(attn_probs * (dprobs - row_dots))
    query_grads = jnp.einsum('hrk,kd->rhd', dscores, keys_f32) * inv_root * factor
    key_part = jnp.einsum('hrk,rhd->kd', dscores, query_f32) * inv_root * factor
    value_part = jnp.einsum('hrk,rhd->kd', probs_low, grad_f32) * factor
    return query_grads.reshape(RESP, QHEADS * HEAD), jnp.concatenate([key_part, value_part], 1)


def reference(queries, resp_kv, out_grad, prompt_key_value, lengths, group_mask):
    token_total = jnp.sum(group_mask[:, None] * lengths)
    factor = (PROMPT_GROUPS * MEMBERS * RESP) / token_total.astype(jnp.float32)

    def live_group(group_index):
        prompt_keys = prompt_key_value[group_index, :, :HEAD]
        prompt_values = prompt_key_value[group_index, :, HEAD:]

        def member_step(prompt_total, member_items):
            query_rows, response_key_value, grad_rows, resp_len = member_items
            live_rows = jnp.arange(RESP) < resp_len
            grad_in = jnp.where(live_rows[:, None], grad_rows, jnp.zeros_like(grad_rows))
            query_grads, kv_parts = member_grads(query_rows, response_key_value, grad_in, prompt_keys, prompt_values, factor)
            return prompt_total + rounded(kv_parts[:PROMPT]), (query_grads.astype(jnp.bfloat16), kv_parts[PROMPT:].astype(jnp.bfloat16))

        member_items = (queries[group_index], resp_kv[group_index], out_grad[group_index], lengths[group_index])
        prompt_total, (query_grads, resp_grads) = lax.scan(member_step, jnp.zeros((PROMPT, 2 * HEAD), jnp.float32), member_items)
        return query_grads, resp_grads, prompt_total.astype(jnp.bfloat16)

    def dead_group(group_index):
        return (jnp.zeros((MEMBERS, RESP, QHEADS * HEAD), jnp.bfloat16),
                jnp.zeros((MEMBERS, RESP, 2 * HEAD), jnp.bfloat16),
                jnp.zeros((PROMPT, 2 * HEAD), jnp.bfloat16))

    def one_group(group_index):
        return lax.cond(group_mask[group_index] > 0, live_group, dead_group, group_index)

    query_grads, resp_grads, prompt_grads = lax.map(one_group, jnp.arange(PROMPT_GROUPS))
    return query_grads, resp_grads, prompt_grads
```

```python
import functools
import math

import jax
import jax.numpy as jnp
from jax import lax
from jax.experimental import pallas as pl
from jax.experimental.pallas import tpu as pltpu
from jax.sharding import PartitionSpec as P

F32, BF16 = jnp.float32, jnp.bfloat16
MESH = pl.DeviceIdType.MESH
SIDE = 4
BLOCK = 128
CHUNK = 2 * BLOCK
LOWEST = -1e30
SUB = 64
SUBS = CHUNK // SUB

ORDER = [(1, 0), (0, 0), (0, 1), (2, 0), (0, 3), (3, 0), (3, 3), (1, 1),
         (2, 3), (1, 3), (0, 2), (2, 1), (3, 1), (3, 2), (1, 2), (2, 2)]
SLOT = {off: i + 2 for i, off in enumerate(ORDER)}
PLACE = {off: i for i, off in enumerate(off for off in ORDER if off != (0, 0))}
CHUNKS = (len(ORDER) + 2) // 2


def shifted(off, way):
    return ((off[0] - way[0]) % SIDE, (off[1] - way[1]) % SIDE)


GATHER = [((0, 0), (far, 0)) for far in (1, -1, 2)]
for i in (1, 0, 3, 2):
    way = 1 if i % 2 == 0 else -1
    GATHER += [((i, 0), (0, way)), ((i, 0), (0, -way)), ((i, -way % SIDE), (0, way))]
LANDS = {shifted(*move): move for move in GATHER}
REDUCE = {to: tuple(step if step == 2 else -step for step in way) for to, (_, way) in LANDS.items()}
TERMS = {off: [o for o in ORDER if o in REDUCE and shifted(o, REDUCE[o]) == off] for off in ORDER}

ARRIVALS = [[], [(3, 0), (1, 0)], [(0, 1), (2, 0)], [(3, 1), (0, 3)], [(3, 3), (1, 1)], [(2, 3), (1, 3)], [(0, 2), (2, 1)],
            [(1, 2), (3, 2)], [(2, 2)]]
DEPARTURES = [[(2, 2), (1, 2)], [(3, 2)], [(2, 1), (0, 2)], [(1, 3), (2, 3)], [(3, 1), (1, 1), (3, 3)], [(0, 3)],
              [(2, 0), (0, 1)], [(3, 0), (1, 0)], []]


def dot(a, b):
    return jnp.dot(a, b, preferred_element_type=F32)


def kernel(dp, heads, rows, scale, q_hbm, rkv_hbm, g_hbm, pkv_hbm, len_ref, mask_ref,
           q_out, r_out, p_out,
           q_ref, qs_ref, graw_ref, gs_ref, qt_ref, gt_ref, kv_ref, kt_ref, p_ref, dp_ref, m_ref, l_ref, d_ref, mh_ref,
           mf_ref, il_ref, rd_ref, dq_ref, part_ref, landed_ref, ak_ref, av_ref, mbuf, fac_ref,
           local_sem, ag_send, ag_recv, rs_send, rs_recv, mask_send, mask_recv):
    me_dp, me = lax.axis_index("dp"), lax.axis_index("group")
    core = me_dp % 2
    strides = (1 + core * (SIDE - 1), SIDE - core * (SIDE - 1))
    places = (me // strides[0] % SIDE, me // strides[1] % SIDE)

    def away(way):
        steps = [(place + step + SIDE) % SIDE - place for place, step in zip(places, way)]
        return (me_dp, me + steps[0] * strides[0] + steps[1] * strides[1])

    near = {way: away(way) for way in dict.fromkeys([w for _, w in GATHER] + list(REDUCE.values()))}
    sibling = (me_dp // 2 * 2 + (1 - me_dp % 2), me)
    above, below = ((me_dp + 2) % dp, me), ((me_dp + dp - 2) % dp, me)
    c2 = scale * math.log2(math.e)

    floor, ring = me_dp // 2, dp // 2
    mbuf[...] = jnp.zeros_like(mbuf)
    barrier = pltpu.get_barrier_semaphore()
    greeted = [*near.values(), sibling]
    for where in greeted:
        pl.semaphore_signal(barrier, inc=1, device_id=where, device_id_type=MESH)

    @pl.when((core == 1) & (floor < ring - 1))
    def _():
        pl.semaphore_signal(barrier, inc=1, device_id=above, device_id_type=MESH)

    @pl.when((core == 1) & (floor > 0))
    def _():
        pl.semaphore_signal(barrier, inc=1, device_id=below, device_id_type=MESH)

    ins = [
        pltpu.make_async_copy(pkv_hbm.at[0], kv_ref.at[pl.ds(SLOT[(0, 0)] * BLOCK, BLOCK)], local_sem.at[0]),
        pltpu.make_async_copy(q_hbm.at[0, 0], q_ref, local_sem.at[1]),
        pltpu.make_async_copy(g_hbm.at[0, 0], graw_ref, local_sem.at[2]),
        pltpu.make_async_copy(rkv_hbm.at[0, 0], kv_ref.at[pl.ds(0, rows)], local_sem.at[3]),
    ]
    for copy in ins:
        copy.start()

    at_end = (floor == 0) | (floor == ring - 1)

    @pl.when((core == 1) & at_end)
    def _():
        pl.semaphore_wait(barrier, len(greeted) + 1)

    @pl.when((core == 1) & jnp.logical_not(at_end))
    def _():
        pl.semaphore_wait(barrier, len(greeted) + 2)

    @pl.when(core == 0)
    def _():
        pl.semaphore_wait(barrier, len(greeted))


    def ag_copy(move):
        off, way = move
        to = shifted(off, way)
        return pltpu.make_async_remote_copy(
            src_ref=kv_ref.at[pl.ds(SLOT[off] * BLOCK, BLOCK)],
            dst_ref=kv_ref.at[pl.ds(SLOT[to] * BLOCK, BLOCK)],
            send_sem=ag_send.at[PLACE[to]],
            recv_sem=ag_recv.at[PLACE[to]],
            device_id=near[way],
            device_id_type=MESH,
        )

    def pass_on(off):
        for move in GATHER:
            if move[0] == off:
                ag_copy(move).start()

    def arrive(off):
        ag_copy(LANDS[off]).wait_recv()
        pass_on(off)

    ins[0].wait()
    pass_on((0, 0))

    most = ring - 1
    every = 3 + 2 * most

    def mask_copy(src, dst, where):
        return pltpu.make_async_remote_copy(
            src_ref=mbuf.at[src],
            dst_ref=mbuf.at[dst],
            send_sem=mask_send.at[dst],
            recv_sem=mask_recv.at[dst],
            device_id=where,
            device_id_type=MESH,
        )

    to_sibling = mask_copy(0, 1, sibling)
    total_back = mask_copy(every, every, sibling)
    lines = [
        ([mask_copy(2 if i == 0 else 2 + i, 3 + i, above) for i in range(most)], floor, most - floor),
        ([mask_copy(2 if i == 0 else 2 + most + i, 3 + most + i, below) for i in range(most)], most - floor, floor),
    ]

    def mask_step(i):
        if i == 0:
            to_sibling.wait_recv()
            mbuf[2] = mbuf[0] + mbuf[1]
        for copies, behind, ahead in lines:
            if i > 0:
                @pl.when(behind >= i)
                def _():
                    copies[i - 1].wait_recv()

            if i < most:
                @pl.when((behind >= i) & (ahead > 0))
                def _():
                    copies[i].start()
        if i == most:
            count = mbuf[2]
            for j in range(2 * most):
                count = count + mbuf[3 + j]
            mbuf[every] = count
            total_back.start()

    mbuf[0] = jnp.broadcast_to(mask_ref[...].astype(F32), (8, 128))

    @pl.when(core == 0)
    def _():
        to_sibling.start()

    m_ref[...] = jnp.full_like(m_ref, LOWEST)
    l_ref[...] = jnp.zeros_like(l_ref)
    d_ref[...] = jnp.zeros_like(d_ref)
    dq_ref[...] = jnp.zeros_like(dq_ref)
    ins[1].wait()
    for h in range(heads):
        q_h = q_ref[:, h * BLOCK : (h + 1) * BLOCK]
        qs_ref[h * rows : (h + 1) * rows, :] = q_h
        qt_ref[h] = q_h.T
    ins[2].wait()
    live = (lax.broadcasted_iota(jnp.int32, (rows, BLOCK), 0) < len_ref[...] * mask_ref[...]).astype(F32)
    for h in range(heads):
        masked = (graw_ref[:, h * BLOCK : (h + 1) * BLOCK].astype(F32) * live).astype(BF16)
        gs_ref[h * rows : (h + 1) * rows, :] = masked
        gt_ref[h] = masked.T
    ins[3].wait()

    def forward_head(c, h, keys, values, allowed):
        s = dot(keys, qt_ref[h])
        if allowed is not None:
            s = jnp.where(allowed, s, LOWEST)
        dprob = dot(values, gt_ref[h])
        dp_ref[c, h] = dprob
        stats = []
        for i in range(SUBS):
            span = slice(i * SUB, (i + 1) * SUB)
            s_i = s[span].reshape(SUB // 8, 8, rows)
            top = jnp.max(s_i, axis=0)
            p = jnp.exp2((s_i - top[None]) * c2)
            total = jnp.sum(p, axis=0)
            weighted = jnp.sum(p * dprob[span].reshape(p.shape), axis=0)
            mh_ref[c, h, i] = top
            p_ref[c, h, span, :] = p.reshape(SUB, rows).astype(BF16)
            stats.append((top, total, weighted))
        m_old = m_ref[h]
        m_new = functools.reduce(jnp.maximum, [top for top, _, _ in stats], m_old)
        fade = jnp.exp2((m_old - m_new) * c2)
        l_new, d_new = l_ref[h] * fade, d_ref[h] * fade
        for top, total, weighted in stats:
            fade = jnp.exp2((top - m_new) * c2)
            l_new, d_new = l_new + total * fade, d_new + weighted * fade
        m_ref[h], l_ref[h], d_ref[h] = m_new, l_new, d_new

    def chunk_kv(c):
        span = pl.ds(pl.multiple_of(c * CHUNK, CHUNK), CHUNK)
        keys, values = kv_ref[span, 0:BLOCK], kv_ref[span, BLOCK : 2 * BLOCK]
        kt_ref[c] = keys.T
        return keys, values

    for off in ARRIVALS[0]:
        arrive(off)

    keys0, values0 = chunk_kv(0)
    allowed = lax.broadcasted_iota(jnp.int32, (CHUNK, rows), 0) <= lax.broadcasted_iota(jnp.int32, (CHUNK, rows), 1)
    for h in range(heads):
        forward_head(0, h, keys0, values0, allowed)

    @pl.loop(1, CHUNKS)
    def _(c):
        for chunk in range(1, CHUNKS):
            @pl.when(c == chunk)
            def _():
                for off in ARRIVALS[chunk]:
                    arrive(off)

        for i in range(4):
            @pl.when((c == 2 * i + 1) & (core == 1))
            def _():
                mask_step(i)

        keys, values = chunk_kv(c)
        for h in range(heads):
            forward_head(c, h, keys, values, None)

    for h in range(heads):
        m = m_ref[h]
        top = jnp.max(m, axis=0, keepdims=True)
        w = jnp.exp2((m - top) * c2)
        inverse = 1.0 / jnp.sum(l_ref[h] * w, axis=0, keepdims=True)
        weighted = jnp.sum(d_ref[h] * w, axis=0, keepdims=True)
        mf_ref[h] = jnp.broadcast_to(top, (8, rows))
        il_ref[h] = jnp.broadcast_to(inverse, (8, rows))
        rd_ref[h] = jnp.broadcast_to(weighted * inverse, (8, rows))

    def rs_copy(off):
        return pltpu.make_async_remote_copy(
            src_ref=part_ref.at[pl.ds(SLOT[off] * BLOCK, BLOCK)],
            dst_ref=landed_ref.at[PLACE[off]],
            send_sem=rs_send.at[PLACE[off]],
            recv_sem=rs_recv.at[PLACE[off]],
            device_id=near[REDUCE[off]],
            device_id_type=MESH,
        )

    def summed(off):
        for o in TERMS[off]:
            rs_copy(o).wait_recv()
        total = part_ref[pl.ds(SLOT[off] * BLOCK, BLOCK), :].astype(F32)
        for o in TERMS[off]:
            total = total + landed_ref[PLACE[o]].astype(F32)
        return total

    def depart(off):
        if TERMS[off]:
            part_ref[pl.ds(SLOT[off] * BLOCK, BLOCK), :] = summed(off).astype(BF16)
        rs_copy(off).start()

    @pl.loop(0, CHUNKS)
    def _(step):
        c = CHUNKS - 1 - step
        k_total = jnp.zeros((CHUNK, BLOCK), F32)
        v_total = jnp.zeros((CHUNK, BLOCK), F32)
        for pair in range(0, heads, 2):
            probs2, dscores2 = [], []
            for h in (pair, pair + 1):
                probs, dscores = [], []
                inverse, row_dots = il_ref[h], rd_ref[h]
                for i in range(SUBS):
                    span = slice(i * SUB, (i + 1) * SUB)
                    share = jnp.exp2((mh_ref[c, h, i] - mf_ref[h]) * c2) * inverse
                    p = p_ref[c, h, span, :].astype(F32).reshape(SUB // 8, 8, rows) * share[None]
                    ds = p * (dp_ref[c, h, span, :].reshape(p.shape) - row_dots[None])
                    probs.append(p.reshape(SUB, rows).astype(BF16))
                    dscores.append(ds.reshape(SUB, rows).astype(BF16))
                probs2.append(jnp.concatenate(probs, axis=0))
                dscores2.append(jnp.concatenate(dscores, axis=0))
                dq_ref[h] = dq_ref[h] + dot(kt_ref[c], dscores2[-1])
            both = slice(pair * rows, (pair + 2) * rows)
            v_total = v_total + dot(jnp.concatenate(probs2, axis=1), gs_ref[both, :])
            k_total = k_total + dot(jnp.concatenate(dscores2, axis=1), qs_ref[both, :])
        ak_ref[...] = k_total
        av_ref[...] = v_total
        span = pl.ds(pl.multiple_of(c * CHUNK, CHUNK), CHUNK)
        part_ref[span, 0:BLOCK] = k_total.astype(BF16)
        part_ref[span, BLOCK : 2 * BLOCK] = v_total.astype(BF16)
        for i in range(4, most + 1):
            @pl.when((step == 2 * (i - 4)) & (core == 1))
            def _():
                mask_step(i)

        for at in range(CHUNKS):
            if DEPARTURES[at]:
                @pl.when(step == at)
                def _():
                    for off in DEPARTURES[at]:
                        depart(off)

    @pl.when(core == 0)
    def _():
        total_back.wait_recv()

    factor = 65536.0 / (mbuf[every] * 3072.0)
    fac_ref[...] = factor
    factor = fac_ref[0:1, :]
    factor_root = factor * scale
    r_out[0, 0, :, 0:BLOCK] = (ak_ref[...] * factor_root).astype(BF16)
    r_out[0, 0, :, BLOCK : 2 * BLOCK] = (av_ref[...] * factor).astype(BF16)
    for h in range(heads):
        q_out[0, 0, :, h * BLOCK : (h + 1) * BLOCK] = (dq_ref[h].T * factor_root).astype(BF16)
    for move in GATHER:
        ag_copy(move).wait_send()
    for off in REDUCE:
        if off not in DEPARTURES[-2]:
            rs_copy(off).wait_send()

    @pl.when(core == 0)
    def _():
        to_sibling.wait_send()

    @pl.when(core == 1)
    def _():
        total_back.wait_send()
        for copies, behind, ahead in lines:
            for i in range(most):
                @pl.when((behind >= i) & (ahead > 0))
                def _():
                    copies[i].wait_send()

    total = summed((0, 0))
    p_out[0, :, 0:BLOCK] = (total[:, 0:BLOCK] * factor_root).astype(BF16)
    p_out[0, :, BLOCK : 2 * BLOCK] = (total[:, BLOCK : 2 * BLOCK] * factor).astype(BF16)
    for off in DEPARTURES[-2]:
        rs_copy(off).wait_send()


def hand_over(*refs):
    count = (len(refs) - 1) // 2
    copies = []
    for src, dst in zip(refs[:count], refs[count:-1]):
        for at in range(0, src.shape[-2], 128):
            place = (*(0,) * (len(src.shape) - 2), pl.ds(at, 128))
            copies.append(pltpu.make_async_copy(src.at[place], dst.at[place], refs[-1].at[len(copies)]))
    for copy in copies:
        copy.start()
    for copy in copies:
        copy.wait()


def on_device(dp, queries, resp_kv, out_grad, prompt_key_value, lengths, group_mask):
    rows = queries.shape[2]
    heads = queries.shape[3] // BLOCK
    keys = CHUNKS * CHUNK
    vmem, sems = pltpu.VMEM, pltpu.SemaphoreType.DMA
    stat = vmem((heads, 8, rows), F32)
    shapes = tuple(jax.ShapeDtypeStruct(a.shape, BF16) for a in (queries, resp_kv, prompt_key_value))
    results = pl.pallas_call(
        functools.partial(kernel, dp, heads, rows, 1.0 / BLOCK**0.5),
        out_shape=tuple(pltpu.VMEM(a.shape, BF16) for a in shapes),
        in_specs=[pl.BlockSpec(memory_space=pl.ANY)] * 4 + [pl.BlockSpec(memory_space=pltpu.VMEM)] * 2,
        out_specs=[pl.BlockSpec(memory_space=pltpu.VMEM)] * 3,
        scratch_shapes=[
            vmem((rows, heads * BLOCK), BF16),
            vmem((heads * rows, BLOCK), BF16),
            vmem((rows, heads * BLOCK), BF16),
            vmem((heads * rows, BLOCK), BF16),
            vmem((heads, BLOCK, rows), BF16),
            vmem((heads, BLOCK, rows), BF16),
            vmem((keys, 2 * BLOCK), BF16),
            vmem((CHUNKS, BLOCK, CHUNK), BF16),
            vmem((CHUNKS, heads, CHUNK, rows), BF16),
            vmem((CHUNKS, heads, CHUNK, rows), F32),
            stat,
            stat,
            stat,
            vmem((CHUNKS, heads, SUBS, 8, rows), F32),
            stat,
            stat,
            stat,
            vmem((heads, BLOCK, rows), F32),
            vmem((keys, 2 * BLOCK), BF16),
            vmem((len(ORDER) - 1, BLOCK, 2 * BLOCK), BF16),
            vmem((CHUNK, BLOCK), F32),
            vmem((CHUNK, BLOCK), F32),
            vmem((dp + 2, 8, 128), F32),
            vmem((8, 128), F32),
            sems((4,)),
            sems((len(ORDER) - 1,)),
            sems((len(ORDER) - 1,)),
            sems((len(ORDER) - 1,)),
            sems((len(ORDER) - 1,)),
            sems((dp + 2,)),
            sems((dp + 2,)),
        ],
        compiler_params=pltpu.CompilerParams(
            collective_id=0, has_side_effects=True, vmem_limit_bytes=58 * 1024 * 1024
        ),
    )(queries, resp_kv, out_grad, prompt_key_value, lengths, group_mask.reshape(1, 1))
    return pl.pallas_call(
        hand_over,
        out_shape=shapes,
        in_specs=[pl.BlockSpec(memory_space=pltpu.VMEM)] * 3,
        out_specs=[pl.BlockSpec(memory_space=pl.ANY)] * 3,
        scratch_shapes=[sems((8,))],
        compiler_params=pltpu.CompilerParams(vmem_limit_bytes=1024 * 1024),
    )(*results)


def solution(mesh):
    in_specs = (
        P("dp", "group", None, None),
        P("dp", "group", None, None),
        P("dp", "group", None, None),
        P("dp", "group", None),
        P("dp", "group"),
        P("dp"),
    )
    out_specs = (P("dp", "group", None, None), P("dp", "group", None, None), P("dp", "group", None))
    return jax.shard_map(
        functools.partial(on_device, mesh.shape["dp"]), mesh=mesh, in_specs=in_specs, out_specs=out_specs, check_vma=False
    )
```

```python
import functools
import math

import jax
import jax.numpy as jnp
from jax import lax
from jax.experimental import pallas as pl
from jax.experimental.pallas import tpu as pltpu
from jax.sharding import PartitionSpec as P

F32, BF16 = jnp.float32, jnp.bfloat16
MESH = pl.DeviceIdType.MESH
SIDE = 4
BLOCK = 128
CHUNK = 2 * BLOCK
LOWEST = -1e30
SUB = 64
SUBS = CHUNK // SUB

ORDER = [(0, 0), (3, 0), (0, 3), (1, 0), (0, 1), (2, 0), (3, 1), (3, 3), (0, 2), (1, 1), (3, 2), (1, 3), (2, 3), (2,
    1), (1, 2), (2, 2)]
SLOT = {off: i + 2 for i, off in enumerate(ORDER)}
PLACE = {off: i for i, off in enumerate(off for off in ORDER if off != (0, 0))}
CHUNKS = (len(ORDER) + 2) // 2


def shifted(off, way):
    return ((off[0] - way[0]) % SIDE, (off[1] - way[1]) % SIDE)


GATHER = [((0, 3), (0, 1)), ((0, 3), (-1, 0)), ((3, 0), (0, -1)), ((0, 0), (1, 0)), ((3, 0), (0, 1)), ((1, 0), (0,
    2)), ((2, 0), (0, 1)), ((2, 0), (0, -1)), ((0, 0), (0, -1)), ((0, 0), (0, 1)), ((0, 0), (-1, 0)), ((3, 2), (1,
    0)), ((0, 0), (2, 0)), ((3, 0), (0, 2)), ((0, 1), (-1, 0))]
SUMS = [((3, 0), (0, 1)), ((1, 0), (0, 1)), ((0, 0), (2, 0)), ((0, 0), (0, -1)), ((3, 0), (0, 2)), ((0, 0), (0, 1)),
    ((2, 0), (0, -1)), ((0, 0), (0, 2)), ((1, 0), (0, -1)), ((0, 0), (1, 0)), ((3, 0), (0, -1)), ((0, 0), (-1, 0)),
    ((2, 0), (0, 2)), ((1, 0), (0, 2)), ((2, 0), (0, 1))]
LANDS = {shifted(*move): move for move in GATHER}
REDUCE = {shifted(*move): tuple(step if step == 2 else -step for step in move[1]) for move in SUMS}
TERMS = {off: [o for o in ORDER if o in REDUCE and shifted(o, REDUCE[o]) == off] for off in ORDER}

ARRIVALS = [[], [(3, 0)], [(0, 1), (0, 3), (1, 0)], [(2, 0)], [(3, 1), (3, 3)], [(3, 2), (0, 2), (1, 1)], [(1, 3)],
    [(2, 3), (2, 1)], [(1, 2), (2, 2)]]
DEPARTURES = [[(2, 2), (1, 2)], [(2, 1), (2, 3)], [(1, 3), (3, 2)], [(1, 1), (0, 2)], [(3, 3), (3, 1)], [(2, 0), (0,
    1)], [(1, 0), (0, 3)], [(3, 0)], []]
LATE = []
LAST = DEPARTURES[-2] + DEPARTURES[-1] + LATE


def dot(a, b):
    return jnp.dot(a, b, preferred_element_type=F32)


def kernel(dp, heads, rows, scale, q_hbm, rkv_hbm, g_hbm, pkv_hbm, len_ref, mask_ref,
           q_out, r_out, p_out,
           q_ref, qs_ref, graw_ref, gs_ref, qt_ref, gt_ref, kv_ref, kt_ref, p_ref, dp_ref, m_ref, l_ref, d_ref, mh_ref,
           mf_ref, il_ref, rd_ref, dq_ref, part_ref, landed_ref, ak_ref, av_ref, mbuf, fac_ref,
           local_sem, ag_send, ag_recv, rs_send, rs_recv, mask_send, mask_recv):
    me_dp, me = lax.axis_index("dp"), lax.axis_index("group")
    core = me_dp % 2
    strides = (1 + core * (SIDE - 1), SIDE - core * (SIDE - 1))
    places = (me // strides[0] % SIDE, me // strides[1] % SIDE)

    def away(way):
        steps = [(place + step + SIDE) % SIDE - place for place, step in zip(places, way)]
        return (me_dp, me + steps[0] * strides[0] + steps[1] * strides[1])

    ways = [way for _, way in GATHER + SUMS]
    ways += [tuple(step if step == 2 else -step for step in way) for way in ways]
    near = {way: away(way) for way in dict.fromkeys(ways)}
    sibling = (me_dp // 2 * 2 + (1 - me_dp % 2), me)
    above, below = ((me_dp + 2) % dp, me), ((me_dp + dp - 2) % dp, me)
    c2 = scale * math.log2(math.e)

    floor, ring = me_dp // 2, dp // 2
    mbuf[...] = jnp.zeros_like(mbuf)
    barrier = pltpu.get_barrier_semaphore()
    greeted = [*near.values(), sibling]
    for where in greeted:
        pl.semaphore_signal(barrier, inc=1, device_id=where, device_id_type=MESH)

    @pl.when((core == 1) & (floor < ring - 1))
    def _():
        pl.semaphore_signal(barrier, inc=1, device_id=above, device_id_type=MESH)

    @pl.when((core == 1) & (floor > 0))
    def _():
        pl.semaphore_signal(barrier, inc=1, device_id=below, device_id_type=MESH)

    ins = [
        pltpu.make_async_copy(pkv_hbm.at[0], kv_ref.at[pl.ds(SLOT[(0, 0)] * BLOCK, BLOCK)], local_sem.at[0]),
        pltpu.make_async_copy(q_hbm.at[0, 0], q_ref, local_sem.at[1]),
        pltpu.make_async_copy(g_hbm.at[0, 0], graw_ref, local_sem.at[2]),
        pltpu.make_async_copy(rkv_hbm.at[0, 0], kv_ref.at[pl.ds(0, rows)], local_sem.at[3]),
    ]
    for copy in ins:
        copy.start()

    at_end = (floor == 0) | (floor == ring - 1)

    @pl.when((core == 1) & at_end)
    def _():
        pl.semaphore_wait(barrier, len(greeted) + 1)

    @pl.when((core == 1) & jnp.logical_not(at_end))
    def _():
        pl.semaphore_wait(barrier, len(greeted) + 2)

    @pl.when(core == 0)
    def _():
        pl.semaphore_wait(barrier, len(greeted))


    def ag_copy(move):
        off, way = move
        to = shifted(off, way)
        return pltpu.make_async_remote_copy(
            src_ref=kv_ref.at[pl.ds(SLOT[off] * BLOCK, BLOCK)],
            dst_ref=kv_ref.at[pl.ds(SLOT[to] * BLOCK, BLOCK)],
            send_sem=ag_send.at[PLACE[to]],
            recv_sem=ag_recv.at[PLACE[to]],
            device_id=near[way],
            device_id_type=MESH,
        )

    def pass_on(off):
        for move in GATHER:
            if move[0] == off:
                ag_copy(move).start()

    def arrive(off):
        ag_copy(LANDS[off]).wait_recv()
        pass_on(off)

    ins[0].wait()
    pass_on((0, 0))

    most = ring - 1
    every = 3 + 2 * most

    def mask_copy(src, dst, where):
        return pltpu.make_async_remote_copy(
            src_ref=mbuf.at[src],
            dst_ref=mbuf.at[dst],
            send_sem=mask_send.at[dst],
            recv_sem=mask_recv.at[dst],
            device_id=where,
            device_id_type=MESH,
        )

    to_sibling = mask_copy(0, 1, sibling)
    total_back = mask_copy(every, every, sibling)
    lines = [
        ([mask_copy(2 if i == 0 else 2 + i, 3 + i, above) for i in range(most)], floor, most - floor),
        ([mask_copy(2 if i == 0 else 2 + most + i, 3 + most + i, below) for i in range(most)], most - floor, floor),
    ]

    def mask_step(i):
        if i == 0:
            to_sibling.wait_recv()
            mbuf[2] = mbuf[0] + mbuf[1]
        for copies, behind, ahead in lines:
            if i > 0:
                @pl.when(behind >= i)
                def _():
                    copies[i - 1].wait_recv()

            if i < most:
                @pl.when((behind >= i) & (ahead > 0))
                def _():
                    copies[i].start()
        if i == most:
            count = mbuf[2]
            for j in range(2 * most):
                count = count + mbuf[3 + j]
            mbuf[every] = count
            total_back.start()

    mbuf[0] = jnp.broadcast_to(mask_ref[...].astype(F32), (8, 128))

    @pl.when(core == 0)
    def _():
        to_sibling.start()

    m_ref[...] = jnp.full_like(m_ref, LOWEST)
    l_ref[...] = jnp.zeros_like(l_ref)
    d_ref[...] = jnp.zeros_like(d_ref)
    dq_ref[...] = jnp.zeros_like(dq_ref)
    ins[1].wait()
    for h in range(heads):
        q_h = q_ref[:, h * BLOCK : (h + 1) * BLOCK]
        qs_ref[h * rows : (h + 1) * rows, :] = q_h
        qt_ref[h] = q_h.T
    ins[2].wait()
    live = (lax.broadcasted_iota(jnp.int32, (rows, BLOCK), 0) < len_ref[...] * mask_ref[...]).astype(F32)
    for h in range(heads):
        masked = (graw_ref[:, h * BLOCK : (h + 1) * BLOCK].astype(F32) * live).astype(BF16)
        gs_ref[h * rows : (h + 1) * rows, :] = masked
        gt_ref[h] = masked.T
    ins[3].wait()

    def forward_head(c, h, keys, values, allowed):
        s = dot(keys, qt_ref[h])
        if allowed is not None:
            s = jnp.where(allowed, s, LOWEST)
        dprob = dot(values, gt_ref[h])
        dp_ref[c, h] = dprob
        stats = []
        for i in range(SUBS):
            span = slice(i * SUB, (i + 1) * SUB)
            s_i = s[span].reshape(SUB // 8, 8, rows)
            top = jnp.max(s_i, axis=0)
            p = jnp.exp2((s_i - top[None]) * c2)
            total = jnp.sum(p, axis=0)
            weighted = jnp.sum(p * dprob[span].reshape(p.shape), axis=0)
            mh_ref[c, h, i] = top
            p_ref[c, h, span, :] = p.reshape(SUB, rows).astype(BF16)
            stats.append((top, total, weighted))
        m_old = m_ref[h]
        m_new = functools.reduce(jnp.maximum, [top for top, _, _ in stats], m_old)
        fade = jnp.exp2((m_old - m_new) * c2)
        l_new, d_new = l_ref[h] * fade, d_ref[h] * fade
        for top, total, weighted in stats:
            fade = jnp.exp2((top - m_new) * c2)
            l_new, d_new = l_new + total * fade, d_new + weighted * fade
        m_ref[h], l_ref[h], d_ref[h] = m_new, l_new, d_new

    def chunk_kv(c):
        span = pl.ds(pl.multiple_of(c * CHUNK, CHUNK), CHUNK)
        keys, values = kv_ref[span, 0:BLOCK], kv_ref[span, BLOCK : 2 * BLOCK]
        kt_ref[c] = keys.T
        return keys, values

    for off in ARRIVALS[0]:
        arrive(off)

    keys0, values0 = chunk_kv(0)
    allowed = lax.broadcasted_iota(jnp.int32, (CHUNK, rows), 0) <= lax.broadcasted_iota(jnp.int32, (CHUNK, rows), 1)
    for h in range(heads):
        forward_head(0, h, keys0, values0, allowed)

    @pl.loop(1, CHUNKS)
    def _(c):
        for chunk in range(1, CHUNKS):
            @pl.when(c == chunk)
            def _():
                for off in ARRIVALS[chunk]:
                    arrive(off)

        for i in range(4):
            @pl.when((c == 2 * i + 1) & (core == 1))
            def _():
                mask_step(i)

        keys, values = chunk_kv(c)
        for h in range(heads):
            forward_head(c, h, keys, values, None)

    for h in range(heads):
        m = m_ref[h]
        top = jnp.max(m, axis=0, keepdims=True)
        w = jnp.exp2((m - top) * c2)
        inverse = 1.0 / jnp.sum(l_ref[h] * w, axis=0, keepdims=True)
        weighted = jnp.sum(d_ref[h] * w, axis=0, keepdims=True)
        mf_ref[h] = jnp.broadcast_to(top, (8, rows))
        il_ref[h] = jnp.broadcast_to(inverse, (8, rows))
        rd_ref[h] = jnp.broadcast_to(weighted * inverse, (8, rows))

    def rs_copy(off):
        return pltpu.make_async_remote_copy(
            src_ref=part_ref.at[pl.ds(SLOT[off] * BLOCK, BLOCK)],
            dst_ref=landed_ref.at[PLACE[off]],
            send_sem=rs_send.at[PLACE[off]],
            recv_sem=rs_recv.at[PLACE[off]],
            device_id=near[REDUCE[off]],
            device_id_type=MESH,
        )

    def summed(off):
        for o in TERMS[off]:
            rs_copy(o).wait_recv()
        total = part_ref[pl.ds(SLOT[off] * BLOCK, BLOCK), :].astype(F32)
        for o in TERMS[off]:
            total = total + landed_ref[PLACE[o]].astype(F32)
        return total

    def depart(off):
        if TERMS[off]:
            part_ref[pl.ds(SLOT[off] * BLOCK, BLOCK), :] = summed(off).astype(BF16)
        rs_copy(off).start()

    @pl.loop(0, CHUNKS)
    def _(step):
        c = CHUNKS - 1 - step
        k_total = jnp.zeros((CHUNK, BLOCK), F32)
        v_total = jnp.zeros((CHUNK, BLOCK), F32)
        for pair in range(0, heads, 2):
            probs2, dscores2 = [], []
            for h in (pair, pair + 1):
                probs, dscores = [], []
                inverse, row_dots = il_ref[h], rd_ref[h]
                for i in range(SUBS):
                    span = slice(i * SUB, (i + 1) * SUB)
                    share = jnp.exp2((mh_ref[c, h, i] - mf_ref[h]) * c2) * inverse
                    p = p_ref[c, h, span, :].astype(F32).reshape(SUB // 8, 8, rows) * share[None]
                    ds = p * (dp_ref[c, h, span, :].reshape(p.shape) - row_dots[None])
                    probs.append(p.reshape(SUB, rows).astype(BF16))
                    dscores.append(ds.reshape(SUB, rows).astype(BF16))
                probs2.append(jnp.concatenate(probs, axis=0))
                dscores2.append(jnp.concatenate(dscores, axis=0))
                dq_ref[h] = dq_ref[h] + dot(kt_ref[c], dscores2[-1])
            both = slice(pair * rows, (pair + 2) * rows)
            v_total = v_total + dot(jnp.concatenate(probs2, axis=1), gs_ref[both, :])
            k_total = k_total + dot(jnp.concatenate(dscores2, axis=1), qs_ref[both, :])
        ak_ref[...] = k_total
        av_ref[...] = v_total
        span = pl.ds(pl.multiple_of(c * CHUNK, CHUNK), CHUNK)
        part_ref[span, 0:BLOCK] = k_total.astype(BF16)
        part_ref[span, BLOCK : 2 * BLOCK] = v_total.astype(BF16)
        for i in range(4, most + 1):
            @pl.when((step == 2 * (i - 4)) & (core == 1))
            def _():
                mask_step(i)

        for at in range(CHUNKS):
            if DEPARTURES[at]:
                @pl.when(step == at)
                def _():
                    for off in DEPARTURES[at]:
                        depart(off)

    for off in LATE:
        depart(off)

    @pl.when(core == 0)
    def _():
        total_back.wait_recv()

    factor = 65536.0 / (mbuf[every] * 3072.0)
    fac_ref[...] = factor
    factor = fac_ref[0:1, :]
    factor_root = factor * scale
    r_out[0, 0, :, 0:BLOCK] = (ak_ref[...] * factor_root).astype(BF16)
    r_out[0, 0, :, BLOCK : 2 * BLOCK] = (av_ref[...] * factor).astype(BF16)
    for h in range(heads):
        q_out[0, 0, :, h * BLOCK : (h + 1) * BLOCK] = (dq_ref[h].T * factor_root).astype(BF16)
    for move in GATHER:
        ag_copy(move).wait_send()
    for off in REDUCE:
        if off not in LAST:
            rs_copy(off).wait_send()

    @pl.when(core == 0)
    def _():
        to_sibling.wait_send()

    @pl.when(core == 1)
    def _():
        total_back.wait_send()
        for copies, behind, ahead in lines:
            for i in range(most):
                @pl.when((behind >= i) & (ahead > 0))
                def _():
                    copies[i].wait_send()

    total = summed((0, 0))
    p_out[0, :, 0:BLOCK] = (total[:, 0:BLOCK] * factor_root).astype(BF16)
    p_out[0, :, BLOCK : 2 * BLOCK] = (total[:, BLOCK : 2 * BLOCK] * factor).astype(BF16)
    for off in LAST:
        rs_copy(off).wait_send()


def hand_over(*refs):
    count = (len(refs) - 1) // 2
    copies = []
    for src, dst in zip(refs[:count], refs[count:-1]):
        for at in range(0, src.shape[-2], 128):
            place = (*(0,) * (len(src.shape) - 2), pl.ds(at, 128))
            copies.append(pltpu.make_async_copy(src.at[place], dst.at[place], refs[-1].at[len(copies)]))
    for copy in copies:
        copy.start()
    for copy in copies:
        copy.wait()


def on_device(dp, queries, resp_kv, out_grad, prompt_key_value, lengths, group_mask):
    rows = queries.shape[2]
    heads = queries.shape[3] // BLOCK
    keys = CHUNKS * CHUNK
    vmem, sems = pltpu.VMEM, pltpu.SemaphoreType.DMA
    stat = vmem((heads, 8, rows), F32)
    shapes = tuple(jax.ShapeDtypeStruct(a.shape, BF16) for a in (queries, resp_kv, prompt_key_value))
    results = pl.pallas_call(
        functools.partial(kernel, dp, heads, rows, 1.0 / BLOCK**0.5),
        out_shape=tuple(pltpu.VMEM(a.shape, BF16) for a in shapes),
        in_specs=[pl.BlockSpec(memory_space=pl.ANY)] * 4 + [pl.BlockSpec(memory_space=pltpu.VMEM)] * 2,
        out_specs=[pl.BlockSpec(memory_space=pltpu.VMEM)] * 3,
        scratch_shapes=[
            vmem((rows, heads * BLOCK), BF16),
            vmem((heads * rows, BLOCK), BF16),
            vmem((rows, heads * BLOCK), BF16),
            vmem((heads * rows, BLOCK), BF16),
            vmem((heads, BLOCK, rows), BF16),
            vmem((heads, BLOCK, rows), BF16),
            vmem((keys, 2 * BLOCK), BF16),
            vmem((CHUNKS, BLOCK, CHUNK), BF16),
            vmem((CHUNKS, heads, CHUNK, rows), BF16),
            vmem((CHUNKS, heads, CHUNK, rows), F32),
            stat,
            stat,
            stat,
            vmem((CHUNKS, heads, SUBS, 8, rows), F32),
            stat,
            stat,
            stat,
            vmem((heads, BLOCK, rows), F32),
            vmem((keys, 2 * BLOCK), BF16),
            vmem((len(ORDER) - 1, BLOCK, 2 * BLOCK), BF16),
            vmem((CHUNK, BLOCK), F32),
            vmem((CHUNK, BLOCK), F32),
            vmem((dp + 2, 8, 128), F32),
            vmem((8, 128), F32),
            sems((4,)),
            sems((len(ORDER) - 1,)),
            sems((len(ORDER) - 1,)),
            sems((len(ORDER) - 1,)),
            sems((len(ORDER) - 1,)),
            sems((dp + 2,)),
            sems((dp + 2,)),
        ],
        compiler_params=pltpu.CompilerParams(
            collective_id=0, has_side_effects=True, vmem_limit_bytes=58 * 1024 * 1024
        ),
    )(queries, resp_kv, out_grad, prompt_key_value, lengths, group_mask.reshape(1, 1))
    return pl.pallas_call(
        hand_over,
        out_shape=shapes,
        in_specs=[pl.BlockSpec(memory_space=pltpu.VMEM)] * 3,
        out_specs=[pl.BlockSpec(memory_space=pl.ANY)] * 3,
        scratch_shapes=[sems((8,))],
        compiler_params=pltpu.CompilerParams(vmem_limit_bytes=1024 * 1024),
    )(*results)


def solution(mesh):
    in_specs = (
        P("dp", "group", None, None),
        P("dp", "group", None, None),
        P("dp", "group", None, None),
        P("dp", "group", None),
        P("dp", "group"),
        P("dp"),
    )
    out_specs = (P("dp", "group", None, None), P("dp", "group", None, None), P("dp", "group", None))
    return jax.shard_map(
        functools.partial(on_device, mesh.shape["dp"]), mesh=mesh, in_specs=in_specs, out_specs=out_specs, check_vma=False
    )
```

```python
import functools
import math

import jax
import jax.numpy as jnp
from jax import lax
from jax.experimental import pallas as pl
from jax.experimental.pallas import tpu as pltpu
from jax.sharding import PartitionSpec as P

F32, BF16 = jnp.float32, jnp.bfloat16
MESH = pl.DeviceIdType.MESH
SIDE = 4
BLOCK = 128
CHUNK = 2 * BLOCK
LOWEST = -1e30
SUB = 64
SUBS = CHUNK // SUB

ORDER = [(0, 0), (3, 0), (0, 3), (1, 0), (0, 1), (2, 0), (3, 1), (3, 3), (0, 2), (1, 1), (3, 2), (1, 3), (2, 3), (2,
    1), (1, 2), (2, 2)]
SLOT = {off: i + 2 for i, off in enumerate(ORDER)}
PLACE = {off: i for i, off in enumerate(off for off in ORDER if off != (0, 0))}
CHUNKS = (len(ORDER) + 2) // 2


def shifted(off, way):
    return ((off[0] - way[0]) % SIDE, (off[1] - way[1]) % SIDE)


GATHER = [((0, 3), (0, 1)), ((0, 3), (-1, 0)), ((3, 0), (0, -1)), ((0, 0), (1, 0)), ((3, 0), (0, 1)), ((1, 0), (0,
    2)), ((2, 0), (0, 1)), ((2, 0), (0, -1)), ((0, 0), (0, -1)), ((0, 0), (0, 1)), ((0, 0), (-1, 0)), ((3, 2), (1,
    0)), ((0, 0), (2, 0)), ((3, 0), (0, 2)), ((0, 1), (-1, 0))]
SUMS = [((3, 0), (0, 1)), ((1, 0), (0, 1)), ((0, 0), (2, 0)), ((0, 0), (0, -1)), ((3, 0), (0, 2)), ((0, 0), (0, 1)),
    ((2, 0), (0, -1)), ((0, 0), (0, 2)), ((1, 0), (0, -1)), ((0, 0), (1, 0)), ((3, 0), (0, -1)), ((0, 0), (-1, 0)),
    ((2, 0), (0, 2)), ((1, 0), (0, 2)), ((2, 0), (0, 1))]
LANDS = {shifted(*move): move for move in GATHER}
REDUCE = {shifted(*move): tuple(step if step == 2 else -step for step in move[1]) for move in SUMS}
TERMS = {off: [o for o in ORDER if o in REDUCE and shifted(o, REDUCE[o]) == off] for off in ORDER}

ARRIVALS = [[], [(3, 0)], [(0, 1), (0, 3), (1, 0)], [(2, 0)], [(3, 1), (3, 3)], [(3, 2), (0, 2), (1, 1)], [(1, 3)],
    [(2, 3), (2, 1)], [(1, 2), (2, 2)]]
DEPARTURES = [[(2, 2), (1, 2)], [(2, 1), (2, 3)], [(1, 3), (3, 2)], [(1, 1), (0, 2)], [(3, 3), (3, 1)], [(2, 0), (0,
    1)], [(1, 0), (0, 3)], [(3, 0)], []]
LATE = []
LAST = DEPARTURES[-2] + DEPARTURES[-1] + LATE


def dot(a, b):
    return jnp.dot(a, b, preferred_element_type=F32)


def kernel(dp, heads, rows, scale, q_hbm, rkv_hbm, g_hbm, pkv_hbm, len_ref, mask_ref,
           q_out, r_out, p_out,
           q_ref, qs_ref, graw_ref, gs_ref, qt_ref, gt_ref, kv_ref, kt_ref, p_ref, dp_ref, m_ref, l_ref, d_ref, mh_ref,
           mf_ref, il_ref, rd_ref, dq_ref, part_ref, landed_ref, ak_ref, av_ref, mbuf, fac_ref,
           local_sem, ag_send, ag_recv, rs_send, rs_recv, mask_send, mask_recv):
    me_dp, me = lax.axis_index("dp"), lax.axis_index("group")
    core = me_dp % 2
    strides = (1 + core * (SIDE - 1), SIDE - core * (SIDE - 1))
    places = (me // strides[0] % SIDE, me // strides[1] % SIDE)

    def away(way):
        steps = [(place + step + SIDE) % SIDE - place for place, step in zip(places, way)]
        return (me_dp, me + steps[0] * strides[0] + steps[1] * strides[1])

    ways = [way for _, way in GATHER + SUMS]
    ways += [tuple(step if step == 2 else -step for step in way) for way in ways]
    near = {way: away(way) for way in dict.fromkeys(ways)}
    sibling = (me_dp // 2 * 2 + (1 - me_dp % 2), me)
    above, below = ((me_dp + 2) % dp, me), ((me_dp + dp - 2) % dp, me)
    c2 = scale * math.log2(math.e)

    floor, ring = me_dp // 2, dp // 2
    mbuf[...] = jnp.zeros_like(mbuf)
    barrier = pltpu.get_barrier_semaphore()
    greeted = [*near.values(), sibling]
    for where in greeted:
        pl.semaphore_signal(barrier, inc=1, device_id=where, device_id_type=MESH)

    @pl.when((core == 1) & (floor < ring - 1))
    def _():
        pl.semaphore_signal(barrier, inc=1, device_id=above, device_id_type=MESH)

    @pl.when((core == 1) & (floor > 0))
    def _():
        pl.semaphore_signal(barrier, inc=1, device_id=below, device_id_type=MESH)

    ins = [
        pltpu.make_async_copy(pkv_hbm.at[0], kv_ref.at[pl.ds(SLOT[(0, 0)] * BLOCK, BLOCK)], local_sem.at[0]),
        pltpu.make_async_copy(q_hbm.at[0, 0], q_ref, local_sem.at[1]),
        pltpu.make_async_copy(g_hbm.at[0, 0], graw_ref, local_sem.at[2]),
        pltpu.make_async_copy(rkv_hbm.at[0, 0], kv_ref.at[pl.ds(0, rows)], local_sem.at[3]),
    ]
    for copy in ins:
        copy.start()

    at_end = (floor == 0) | (floor == ring - 1)

    @pl.when((core == 1) & at_end)
    def _():
        pl.semaphore_wait(barrier, len(greeted) + 1)

    @pl.when((core == 1) & jnp.logical_not(at_end))
    def _():
        pl.semaphore_wait(barrier, len(greeted) + 2)

    @pl.when(core == 0)
    def _():
        pl.semaphore_wait(barrier, len(greeted))


    def ag_copy(move):
        off, way = move
        to = shifted(off, way)
        return pltpu.make_async_remote_copy(
            src_ref=kv_ref.at[pl.ds(SLOT[off] * BLOCK, BLOCK)],
            dst_ref=kv_ref.at[pl.ds(SLOT[to] * BLOCK, BLOCK)],
            send_sem=ag_send.at[PLACE[to]],
            recv_sem=ag_recv.at[PLACE[to]],
            device_id=near[way],
            device_id_type=MESH,
        )

    def pass_on(off):
        for move in GATHER:
            if move[0] == off:
                ag_copy(move).start()

    def arrive(off):
        ag_copy(LANDS[off]).wait_recv()
        pass_on(off)

    ins[0].wait()
    pass_on((0, 0))

    most = ring - 1
    every = 3 + 2 * most

    def mask_copy(src, dst, where):
        return pltpu.make_async_remote_copy(
            src_ref=mbuf.at[src],
            dst_ref=mbuf.at[dst],
            send_sem=mask_send.at[dst],
            recv_sem=mask_recv.at[dst],
            device_id=where,
            device_id_type=MESH,
        )

    to_sibling = mask_copy(0, 1, sibling)
    total_back = mask_copy(every, every, sibling)
    lines = [
        ([mask_copy(2 if i == 0 else 2 + i, 3 + i, above) for i in range(most)], floor, most - floor),
        ([mask_copy(2 if i == 0 else 2 + most + i, 3 + most + i, below) for i in range(most)], most - floor, floor),
    ]

    def mask_step(i):
        if i == 0:
            to_sibling.wait_recv()
            mbuf[2] = mbuf[0] + mbuf[1]
        for copies, behind, ahead in lines:
            if i > 0:
                @pl.when(behind >= i)
                def _():
                    copies[i - 1].wait_recv()

            if i < most:
                @pl.when((behind >= i) & (ahead > 0))
                def _():
                    copies[i].start()
        if i == most:
            count = mbuf[2]
            for j in range(2 * most):
                count = count + mbuf[3 + j]
            mbuf[every] = count
            total_back.start()

    mbuf[0] = jnp.broadcast_to(mask_ref[...].astype(F32), (8, 128))

    @pl.when(core == 0)
    def _():
        to_sibling.start()

    m_ref[...] = jnp.full_like(m_ref, LOWEST)
    l_ref[...] = jnp.zeros_like(l_ref)
    d_ref[...] = jnp.zeros_like(d_ref)
    dq_ref[...] = jnp.zeros_like(dq_ref)
    ins[1].wait()
    for h in range(heads):
        q_h = q_ref[:, h * BLOCK : (h + 1) * BLOCK]
        qs_ref[h * rows : (h + 1) * rows, :] = q_h
        qt_ref[h] = q_h.T
    ins[2].wait()
    live = (lax.broadcasted_iota(jnp.int32, (rows, BLOCK), 0) < len_ref[...] * mask_ref[...]).astype(F32)
    for h in range(heads):
        masked = (graw_ref[:, h * BLOCK : (h + 1) * BLOCK].astype(F32) * live).astype(BF16)
        gs_ref[h * rows : (h + 1) * rows, :] = masked
        gt_ref[h] = masked.T
    ins[3].wait()

    def forward_head(c, h, keys, values, allowed):
        s = dot(keys, qt_ref[h])
        if allowed is not None:
            s = jnp.where(allowed, s, LOWEST)
        dprob = dot(values, gt_ref[h])
        dp_ref[c, h] = dprob
        stats = []
        for i in range(SUBS):
            span = slice(i * SUB, (i + 1) * SUB)
            s_i = s[span].reshape(SUB // 8, 8, rows)
            top = jnp.max(s_i, axis=0)
            p = jnp.exp2((s_i - top[None]) * c2)
            total = jnp.sum(p, axis=0)
            weighted = jnp.sum(p * dprob[span].reshape(p.shape), axis=0)
            mh_ref[c, h, i] = top
            p_ref[c, h, span, :] = p.reshape(SUB, rows).astype(BF16)
            stats.append((top, total, weighted))
        m_old = m_ref[h]
        m_new = functools.reduce(jnp.maximum, [top for top, _, _ in stats], m_old)
        fade = jnp.exp2((m_old - m_new) * c2)
        l_new, d_new = l_ref[h] * fade, d_ref[h] * fade
        for top, total, weighted in stats:
            fade = jnp.exp2((top - m_new) * c2)
            l_new, d_new = l_new + total * fade, d_new + weighted * fade
        m_ref[h], l_ref[h], d_ref[h] = m_new, l_new, d_new

    def chunk_kv(c):
        span = pl.ds(pl.multiple_of(c * CHUNK, CHUNK), CHUNK)
        keys, values = kv_ref[span, 0:BLOCK], kv_ref[span, BLOCK : 2 * BLOCK]
        kt_ref[c] = keys.T
        return keys, values

    for off in ARRIVALS[0]:
        arrive(off)

    keys0, values0 = chunk_kv(0)
    allowed = lax.broadcasted_iota(jnp.int32, (CHUNK, rows), 0) <= lax.broadcasted_iota(jnp.int32, (CHUNK, rows), 1)
    for h in range(heads):
        forward_head(0, h, keys0, values0, allowed)

    @pl.loop(1, CHUNKS)
    def _(c):
        for chunk in range(1, CHUNKS):
            @pl.when(c == chunk)
            def _():
                for off in ARRIVALS[chunk]:
                    arrive(off)

        for i in range(4):
            @pl.when((c == 2 * i + 1) & (core == 1))
            def _():
                mask_step(i)

        keys, values = chunk_kv(c)
        for h in range(heads):
            forward_head(c, h, keys, values, None)

    for h in range(heads):
        m = m_ref[h]
        top = jnp.max(m, axis=0, keepdims=True)
        w = jnp.exp2((m - top) * c2)
        inverse = 1.0 / jnp.sum(l_ref[h] * w, axis=0, keepdims=True)
        weighted = jnp.sum(d_ref[h] * w, axis=0, keepdims=True)
        mf_ref[h] = jnp.broadcast_to(top, (8, rows))
        il_ref[h] = jnp.broadcast_to(inverse, (8, rows))
        rd_ref[h] = jnp.broadcast_to(weighted * inverse, (8, rows))

    def rs_copy(off):
        return pltpu.make_async_remote_copy(
            src_ref=part_ref.at[pl.ds(SLOT[off] * BLOCK, BLOCK)],
            dst_ref=landed_ref.at[PLACE[off]],
            send_sem=rs_send.at[PLACE[off]],
            recv_sem=rs_recv.at[PLACE[off]],
            device_id=near[REDUCE[off]],
            device_id_type=MESH,
        )

    def summed(off):
        for o in TERMS[off]:
            rs_copy(o).wait_recv()
        total = part_ref[pl.ds(SLOT[off] * BLOCK, BLOCK), :].astype(F32)
        for o in TERMS[off]:
            total = total + landed_ref[PLACE[o]].astype(F32)
        return total

    def depart(off):
        if TERMS[off]:
            part_ref[pl.ds(SLOT[off] * BLOCK, BLOCK), :] = summed(off).astype(BF16)
        rs_copy(off).start()

    @pl.loop(0, CHUNKS)
    def _(step):
        c = CHUNKS - 1 - step
        k_total = jnp.zeros((CHUNK, BLOCK), F32)
        v_total = jnp.zeros((CHUNK, BLOCK), F32)
        for pair in range(0, heads, 2):
            probs2, dscores2 = [], []
            for h in (pair, pair + 1):
                probs, dscores = [], []
                inverse, row_dots = il_ref[h], rd_ref[h]
                for i in range(SUBS):
                    span = slice(i * SUB, (i + 1) * SUB)
                    share = jnp.exp2((mh_ref[c, h, i] - mf_ref[h]) * c2) * inverse
                    share = jnp.concatenate([share, share], axis=0).astype(BF16)
                    p = (p_ref[c, h, span, :].reshape(SUB // 16, 16, rows) * share[None]).reshape(SUB, rows)
                    ds = dp_ref[c, h, span, :].reshape(SUB // 8, 8, rows) - row_dots[None]
                    ds = p.astype(F32) * ds.reshape(SUB, rows)
                    probs.append(p)
                    dscores.append(ds.astype(BF16))
                probs2.append(jnp.concatenate(probs, axis=0))
                dscores2.append(jnp.concatenate(dscores, axis=0))
                dq_ref[h] = dq_ref[h] + dot(kt_ref[c], dscores2[-1])
            both = slice(pair * rows, (pair + 2) * rows)
            v_total = v_total + dot(jnp.concatenate(probs2, axis=1), gs_ref[both, :])
            k_total = k_total + dot(jnp.concatenate(dscores2, axis=1), qs_ref[both, :])
        ak_ref[...] = k_total
        av_ref[...] = v_total
        span = pl.ds(pl.multiple_of(c * CHUNK, CHUNK), CHUNK)
        part_ref[span, 0:BLOCK] = k_total.astype(BF16)
        part_ref[span, BLOCK : 2 * BLOCK] = v_total.astype(BF16)
        for i in range(4, most + 1):
            @pl.when((step == 2 * (i - 4)) & (core == 1))
            def _():
                mask_step(i)

        for at in range(CHUNKS):
            if DEPARTURES[at]:
                @pl.when(step == at)
                def _():
                    for off in DEPARTURES[at]:
                        depart(off)

    for off in LATE:
        depart(off)

    @pl.when(core == 0)
    def _():
        total_back.wait_recv()

    factor = 65536.0 / (mbuf[every] * 3072.0)
    fac_ref[...] = factor
    factor = fac_ref[0:1, :]
    factor_root = factor * scale
    r_out[0, 0, :, 0:BLOCK] = (ak_ref[...] * factor_root).astype(BF16)
    r_out[0, 0, :, BLOCK : 2 * BLOCK] = (av_ref[...] * factor).astype(BF16)
    for h in range(heads):
        q_out[0, 0, :, h * BLOCK : (h + 1) * BLOCK] = (dq_ref[h].T * factor_root).astype(BF16)
    for move in GATHER:
        ag_copy(move).wait_send()
    for off in REDUCE:
        if off not in LAST:
            rs_copy(off).wait_send()

    @pl.when(core == 0)
    def _():
        to_sibling.wait_send()

    @pl.when(core == 1)
    def _():
        total_back.wait_send()
        for copies, behind, ahead in lines:
            for i in range(most):
                @pl.when((behind >= i) & (ahead > 0))
                def _():
                    copies[i].wait_send()

    total = summed((0, 0))
    p_out[0, :, 0:BLOCK] = (total[:, 0:BLOCK] * factor_root).astype(BF16)
    p_out[0, :, BLOCK : 2 * BLOCK] = (total[:, BLOCK : 2 * BLOCK] * factor).astype(BF16)
    for off in LAST:
        rs_copy(off).wait_send()


def hand_over(*refs):
    count = (len(refs) - 1) // 2
    copies = []
    for src, dst in zip(refs[:count], refs[count:-1]):
        for at in range(0, src.shape[-2], 128):
            place = (*(0,) * (len(src.shape) - 2), pl.ds(at, 128))
            copies.append(pltpu.make_async_copy(src.at[place], dst.at[place], refs[-1].at[len(copies)]))
    for copy in copies:
        copy.start()
    for copy in copies:
        copy.wait()


def on_device(dp, queries, resp_kv, out_grad, prompt_key_value, lengths, group_mask):
    rows = queries.shape[2]
    heads = queries.shape[3] // BLOCK
    keys = CHUNKS * CHUNK
    vmem, sems = pltpu.VMEM, pltpu.SemaphoreType.DMA
    stat = vmem((heads, 8, rows), F32)
    shapes = tuple(jax.ShapeDtypeStruct(a.shape, BF16) for a in (queries, resp_kv, prompt_key_value))
    results = pl.pallas_call(
        functools.partial(kernel, dp, heads, rows, 1.0 / BLOCK**0.5),
        out_shape=tuple(pltpu.VMEM(a.shape, BF16) for a in shapes),
        in_specs=[pl.BlockSpec(memory_space=pl.ANY)] * 4 + [pl.BlockSpec(memory_space=pltpu.VMEM)] * 2,
        out_specs=[pl.BlockSpec(memory_space=pltpu.VMEM)] * 3,
        scratch_shapes=[
            vmem((rows, heads * BLOCK), BF16),
            vmem((heads * rows, BLOCK), BF16),
            vmem((rows, heads * BLOCK), BF16),
            vmem((heads * rows, BLOCK), BF16),
            vmem((heads, BLOCK, rows), BF16),
            vmem((heads, BLOCK, rows), BF16),
            vmem((keys, 2 * BLOCK), BF16),
            vmem((CHUNKS, BLOCK, CHUNK), BF16),
            vmem((CHUNKS, heads, CHUNK, rows), BF16),
            vmem((CHUNKS, heads, CHUNK, rows), F32),
            stat,
            stat,
            stat,
            vmem((CHUNKS, heads, SUBS, 8, rows), F32),
            stat,
            stat,
            stat,
            vmem((heads, BLOCK, rows), F32),
            vmem((keys, 2 * BLOCK), BF16),
            vmem((len(ORDER) - 1, BLOCK, 2 * BLOCK), BF16),
            vmem((CHUNK, BLOCK), F32),
            vmem((CHUNK, BLOCK), F32),
            vmem((dp + 2, 8, 128), F32),
            vmem((8, 128), F32),
            sems((4,)),
            sems((len(ORDER) - 1,)),
            sems((len(ORDER) - 1,)),
            sems((len(ORDER) - 1,)),
            sems((len(ORDER) - 1,)),
            sems((dp + 2,)),
            sems((dp + 2,)),
        ],
        compiler_params=pltpu.CompilerParams(
            collective_id=0, has_side_effects=True, vmem_limit_bytes=58 * 1024 * 1024
        ),
    )(queries, resp_kv, out_grad, prompt_key_value, lengths, group_mask.reshape(1, 1))
    return pl.pallas_call(
        hand_over,
        out_shape=shapes,
        in_specs=[pl.BlockSpec(memory_space=pltpu.VMEM)] * 3,
        out_specs=[pl.BlockSpec(memory_space=pl.ANY)] * 3,
        scratch_shapes=[sems((8,))],
        compiler_params=pltpu.CompilerParams(vmem_limit_bytes=1024 * 1024),
    )(*results)


def solution(mesh):
    in_specs = (
        P("dp", "group", None, None),
        P("dp", "group", None, None),
        P("dp", "group", None, None),
        P("dp", "group", None),
        P("dp", "group"),
        P("dp"),
    )
    out_specs = (P("dp", "group", None, None), P("dp", "group", None, None), P("dp", "group", None))
    return jax.shard_map(
        functools.partial(on_device, mesh.shape["dp"]), mesh=mesh, in_specs=in_specs, out_specs=out_specs, check_vma=False
    )
```

```python
import functools
import math

import jax
import jax.numpy as jnp
from jax import lax
from jax.experimental import pallas as pl
from jax.experimental.pallas import tpu as pltpu
from jax.sharding import PartitionSpec as P

F32, BF16 = jnp.float32, jnp.bfloat16
MESH = pl.DeviceIdType.MESH
SIDE = 4
BLOCK = 128
CHUNK = 2 * BLOCK
LOWEST = -1e30
SUB = 64
SUBS = CHUNK // SUB

ORDER = [(0, 0), (3, 0), (0, 3), (1, 0), (0, 1), (2, 0), (3, 1), (3, 3), (0, 2), (1, 1), (3, 2), (1, 3), (2, 3), (2,
    1), (1, 2), (2, 2)]
SLOT = {off: i + 2 for i, off in enumerate(ORDER)}
PLACE = {off: i for i, off in enumerate(off for off in ORDER if off != (0, 0))}
CHUNKS = (len(ORDER) + 2) // 2


def shifted(off, way):
    return ((off[0] - way[0]) % SIDE, (off[1] - way[1]) % SIDE)


GATHER = [((0, 3), (0, 1)), ((0, 3), (-1, 0)), ((3, 0), (0, -1)), ((0, 0), (1, 0)), ((3, 0), (0, 1)), ((1, 0), (0,
    2)), ((2, 0), (0, 1)), ((2, 0), (0, -1)), ((0, 0), (0, -1)), ((0, 0), (0, 1)), ((0, 0), (-1, 0)), ((3, 2), (1,
    0)), ((0, 0), (2, 0)), ((3, 0), (0, 2)), ((0, 1), (-1, 0))]
SUMS = [((3, 0), (0, 1)), ((1, 0), (0, 1)), ((0, 0), (2, 0)), ((0, 0), (0, -1)), ((3, 0), (0, 2)), ((0, 0), (0, 1)),
    ((2, 0), (0, -1)), ((0, 0), (0, 2)), ((1, 0), (0, -1)), ((0, 0), (1, 0)), ((3, 0), (0, -1)), ((0, 0), (-1, 0)),
    ((2, 0), (0, 2)), ((1, 0), (0, 2)), ((2, 0), (0, 1))]
LANDS = {shifted(*move): move for move in GATHER}
REDUCE = {shifted(*move): tuple(step if step == 2 else -step for step in move[1]) for move in SUMS}
TERMS = {off: [o for o in ORDER if o in REDUCE and shifted(o, REDUCE[o]) == off] for off in ORDER}

ARRIVALS = [[], [(3, 0)], [(0, 1), (0, 3), (1, 0)], [(2, 0)], [(3, 1), (3, 3)], [(3, 2), (0, 2), (1, 1)], [(1, 3)],
    [(2, 3), (2, 1)], [(1, 2), (2, 2)]]
DEPARTURES = [[(2, 2), (1, 2)], [(2, 1), (2, 3)], [(1, 3), (3, 2)], [(1, 1), (0, 2)], [(3, 3), (3, 1)], [(2, 0), (0,
    1)], [(1, 0), (0, 3)], [(3, 0)], []]
LATE = []
LAST = DEPARTURES[-2] + DEPARTURES[-1] + LATE


def choose(index, low, actions):
    if len(actions) == 1:
        actions[0]()
        return
    half = len(actions) // 2
    lax.cond(
        index < low + half,
        lambda: choose(index, low, actions[:half]),
        lambda: choose(index, low + half, actions[half:]),
    )


def dot(a, b):
    return jnp.dot(a, b, preferred_element_type=F32)


def kernel(dp, heads, rows, scale, q_hbm, rkv_hbm, g_hbm, pkv_hbm, len_ref, mask_ref,
           q_out, r_out, p_out,
           q_ref, qs_ref, graw_ref, gs_ref, qt_ref, gt_ref, kv_ref, kt_ref, p_ref, dp_ref, m_ref, l_ref, d_ref, mh_ref,
           mf_ref, il_ref, rd_ref, dq_ref, part_ref, landed_ref, ak_ref, av_ref, mbuf, fac_ref,
           local_sem, ag_send, ag_recv, rs_send, rs_recv, mask_send, mask_recv):
    me_dp, me = lax.axis_index("dp"), lax.axis_index("group")
    core = me_dp % 2
    strides = (1 + core * (SIDE - 1), SIDE - core * (SIDE - 1))
    places = (me // strides[0] % SIDE, me // strides[1] % SIDE)

    def away(way):
        steps = [(place + step + SIDE) % SIDE - place for place, step in zip(places, way)]
        return (me_dp, me + steps[0] * strides[0] + steps[1] * strides[1])

    ways = [way for _, way in GATHER + SUMS]
    ways += [tuple(step if step == 2 else -step for step in way) for way in ways]
    near = {way: away(way) for way in dict.fromkeys(ways)}
    sibling = (me_dp // 2 * 2 + (1 - me_dp % 2), me)
    above, below = ((me_dp + 2) % dp, me), ((me_dp + dp - 2) % dp, me)
    c2 = scale * math.log2(math.e)

    floor, ring = me_dp // 2, dp // 2
    mbuf[...] = jnp.zeros_like(mbuf)
    barrier = pltpu.get_barrier_semaphore()
    greeted = [*near.values(), sibling]
    for where in greeted:
        pl.semaphore_signal(barrier, inc=1, device_id=where, device_id_type=MESH)

    @pl.when((core == 1) & (floor < ring - 1))
    def _():
        pl.semaphore_signal(barrier, inc=1, device_id=above, device_id_type=MESH)

    @pl.when((core == 1) & (floor > 0))
    def _():
        pl.semaphore_signal(barrier, inc=1, device_id=below, device_id_type=MESH)

    ins = [
        pltpu.make_async_copy(pkv_hbm.at[0], kv_ref.at[pl.ds(SLOT[(0, 0)] * BLOCK, BLOCK)], local_sem.at[0]),
        pltpu.make_async_copy(q_hbm.at[0, 0], q_ref, local_sem.at[1]),
        pltpu.make_async_copy(g_hbm.at[0, 0], graw_ref, local_sem.at[2]),
        pltpu.make_async_copy(rkv_hbm.at[0, 0], kv_ref.at[pl.ds(0, rows)], local_sem.at[3]),
    ]
    for copy in ins:
        copy.start()

    at_end = (floor == 0) | (floor == ring - 1)

    @pl.when((core == 1) & at_end)
    def _():
        pl.semaphore_wait(barrier, len(greeted) + 1)

    @pl.when((core == 1) & jnp.logical_not(at_end))
    def _():
        pl.semaphore_wait(barrier, len(greeted) + 2)

    @pl.when(core == 0)
    def _():
        pl.semaphore_wait(barrier, len(greeted))


    def ag_copy(move):
        off, way = move
        to = shifted(off, way)
        return pltpu.make_async_remote_copy(
            src_ref=kv_ref.at[pl.ds(SLOT[off] * BLOCK, BLOCK)],
            dst_ref=kv_ref.at[pl.ds(SLOT[to] * BLOCK, BLOCK)],
            send_sem=ag_send.at[PLACE[to]],
            recv_sem=ag_recv.at[PLACE[to]],
            device_id=near[way],
            device_id_type=MESH,
        )

    def pass_on(off):
        for move in GATHER:
            if move[0] == off:
                ag_copy(move).start()

    def arrive(off):
        ag_copy(LANDS[off]).wait_recv()
        pass_on(off)

    ins[0].wait()
    pass_on((0, 0))

    most = ring - 1
    every = 3 + 2 * most

    def mask_copy(src, dst, where):
        return pltpu.make_async_remote_copy(
            src_ref=mbuf.at[src],
            dst_ref=mbuf.at[dst],
            send_sem=mask_send.at[dst],
            recv_sem=mask_recv.at[dst],
            device_id=where,
            device_id_type=MESH,
        )

    to_sibling = mask_copy(0, 1, sibling)
    total_back = mask_copy(every, every, sibling)
    lines = [
        ([mask_copy(2 if i == 0 else 2 + i, 3 + i, above) for i in range(most)], floor, most - floor),
        ([mask_copy(2 if i == 0 else 2 + most + i, 3 + most + i, below) for i in range(most)], most - floor, floor),
    ]

    def mask_step(i):
        if i == 0:
            to_sibling.wait_recv()
            mbuf[2] = mbuf[0] + mbuf[1]
        for copies, behind, ahead in lines:
            if i > 0:
                @pl.when(behind >= i)
                def _():
                    copies[i - 1].wait_recv()

            if i < most:
                @pl.when((behind >= i) & (ahead > 0))
                def _():
                    copies[i].start()
        if i == most:
            count = mbuf[2]
            for j in range(2 * most):
                count = count + mbuf[3 + j]
            mbuf[every] = count
            total_back.start()

    mbuf[0] = jnp.broadcast_to(mask_ref[...].astype(F32), (8, 128))

    @pl.when(core == 0)
    def _():
        to_sibling.start()

    m_ref[...] = jnp.full_like(m_ref, LOWEST)
    l_ref[...] = jnp.zeros_like(l_ref)
    d_ref[...] = jnp.zeros_like(d_ref)
    dq_ref[...] = jnp.zeros_like(dq_ref)
    ins[1].wait()
    for h in range(heads):
        q_h = q_ref[:, h * BLOCK : (h + 1) * BLOCK]
        qs_ref[h * rows : (h + 1) * rows, :] = q_h
        qt_ref[h] = q_h.T
    ins[2].wait()
    live = (lax.broadcasted_iota(jnp.int32, (rows, BLOCK), 0) < len_ref[...] * mask_ref[...]).astype(F32)
    for h in range(heads):
        masked = (graw_ref[:, h * BLOCK : (h + 1) * BLOCK].astype(F32) * live).astype(BF16)
        gs_ref[h * rows : (h + 1) * rows, :] = masked
        gt_ref[h] = masked.T
    ins[3].wait()

    def forward_head(c, h, keys, values, allowed):
        s = dot(keys, qt_ref[h])
        if allowed is not None:
            s = jnp.where(allowed, s, LOWEST)
        dprob = dot(values, gt_ref[h])
        dp_ref[c, h] = dprob
        stats = []
        for i in range(SUBS):
            span = slice(i * SUB, (i + 1) * SUB)
            s_i = s[span].reshape(SUB // 8, 8, rows)
            top = jnp.max(s_i, axis=0)
            p = jnp.exp2((s_i - top[None]) * c2)
            total = jnp.sum(p, axis=0)
            weighted = jnp.sum(p * dprob[span].reshape(p.shape), axis=0)
            mh_ref[c, h, i] = top
            p_ref[c, h, span, :] = p.reshape(SUB, rows).astype(BF16)
            stats.append((top, total, weighted))
        m_old = m_ref[h]
        m_new = functools.reduce(jnp.maximum, [top for top, _, _ in stats], m_old)
        fade = jnp.exp2((m_old - m_new) * c2)
        l_new, d_new = l_ref[h] * fade, d_ref[h] * fade
        for top, total, weighted in stats:
            fade = jnp.exp2((top - m_new) * c2)
            l_new, d_new = l_new + total * fade, d_new + weighted * fade
        m_ref[h], l_ref[h], d_ref[h] = m_new, l_new, d_new

    def chunk_kv(c):
        span = pl.ds(pl.multiple_of(c * CHUNK, CHUNK), CHUNK)
        keys, values = kv_ref[span, 0:BLOCK], kv_ref[span, BLOCK : 2 * BLOCK]
        kt_ref[c] = keys.T
        return keys, values

    for off in ARRIVALS[0]:
        arrive(off)

    keys0, values0 = chunk_kv(0)
    allowed = lax.broadcasted_iota(jnp.int32, (CHUNK, rows), 0) <= lax.broadcasted_iota(jnp.int32, (CHUNK, rows), 1)
    for h in range(heads):
        forward_head(0, h, keys0, values0, allowed)

    @pl.loop(1, CHUNKS)
    def _(c):
        def before(chunk):
            for off in ARRIVALS[chunk]:
                arrive(off)
            if chunk in (1, 3, 5, 7):
                @pl.when(core == 1)
                def _():
                    mask_step(chunk // 2)

        choose(c, 1, [functools.partial(before, chunk) for chunk in range(1, CHUNKS)])
        keys, values = chunk_kv(c)
        for h in range(heads):
            forward_head(c, h, keys, values, None)

    for h in range(heads):
        m = m_ref[h]
        top = jnp.max(m, axis=0, keepdims=True)
        w = jnp.exp2((m - top) * c2)
        inverse = 1.0 / jnp.sum(l_ref[h] * w, axis=0, keepdims=True)
        weighted = jnp.sum(d_ref[h] * w, axis=0, keepdims=True)
        mf_ref[h] = jnp.broadcast_to(top, (8, rows))
        il_ref[h] = jnp.broadcast_to(inverse, (8, rows))
        rd_ref[h] = jnp.broadcast_to(weighted * inverse, (8, rows))

    def rs_copy(off):
        return pltpu.make_async_remote_copy(
            src_ref=part_ref.at[pl.ds(SLOT[off] * BLOCK, BLOCK)],
            dst_ref=landed_ref.at[PLACE[off]],
            send_sem=rs_send.at[PLACE[off]],
            recv_sem=rs_recv.at[PLACE[off]],
            device_id=near[REDUCE[off]],
            device_id_type=MESH,
        )

    def summed(off):
        for o in TERMS[off]:
            rs_copy(o).wait_recv()
        total = part_ref[pl.ds(SLOT[off] * BLOCK, BLOCK), :].astype(F32)
        for o in TERMS[off]:
            total = total + landed_ref[PLACE[o]].astype(F32)
        return total

    def depart(off):
        if TERMS[off]:
            part_ref[pl.ds(SLOT[off] * BLOCK, BLOCK), :] = summed(off).astype(BF16)
        rs_copy(off).start()

    @pl.loop(0, CHUNKS)
    def _(step):
        c = CHUNKS - 1 - step
        k_total = jnp.zeros((CHUNK, BLOCK), F32)
        v_total = jnp.zeros((CHUNK, BLOCK), F32)
        for pair in range(0, heads, 2):
            probs2, dscores2 = [], []
            for h in (pair, pair + 1):
                probs, dscores = [], []
                inverse, row_dots = il_ref[h], rd_ref[h]
                for i in range(SUBS):
                    span = slice(i * SUB, (i + 1) * SUB)
                    share = jnp.exp2((mh_ref[c, h, i] - mf_ref[h]) * c2) * inverse
                    p = p_ref[c, h, span, :].astype(F32).reshape(SUB // 8, 8, rows) * share[None]
                    ds = p * (dp_ref[c, h, span, :].reshape(p.shape) - row_dots[None])
                    probs.append(p.reshape(SUB, rows).astype(BF16))
                    dscores.append(ds.reshape(SUB, rows).astype(BF16))
                probs2.append(jnp.concatenate(probs, axis=0))
                dscores2.append(jnp.concatenate(dscores, axis=0))
                dq_ref[h] = dq_ref[h] + dot(kt_ref[c], dscores2[-1])
            both = slice(pair * rows, (pair + 2) * rows)
            v_total = v_total + dot(jnp.concatenate(probs2, axis=1), gs_ref[both, :])
            k_total = k_total + dot(jnp.concatenate(dscores2, axis=1), qs_ref[both, :])
        ak_ref[...] = k_total
        av_ref[...] = v_total
        span = pl.ds(pl.multiple_of(c * CHUNK, CHUNK), CHUNK)
        part_ref[span, 0:BLOCK] = k_total.astype(BF16)
        part_ref[span, BLOCK : 2 * BLOCK] = v_total.astype(BF16)

        def after(at):
            if at % 2 == 0 and 4 + at // 2 <= most:
                @pl.when(core == 1)
                def _():
                    mask_step(4 + at // 2)

            for off in DEPARTURES[at]:
                depart(off)

        choose(step, 0, [functools.partial(after, at) for at in range(CHUNKS)])

    for off in LATE:
        depart(off)

    @pl.when(core == 0)
    def _():
        total_back.wait_recv()

    factor = 65536.0 / (mbuf[every] * 3072.0)
    fac_ref[...] = factor
    factor = fac_ref[0:1, :]
    factor_root = factor * scale
    r_out[0, 0, :, 0:BLOCK] = (ak_ref[...] * factor_root).astype(BF16)
    r_out[0, 0, :, BLOCK : 2 * BLOCK] = (av_ref[...] * factor).astype(BF16)
    for h in range(heads):
        q_out[0, 0, :, h * BLOCK : (h + 1) * BLOCK] = (dq_ref[h].T * factor_root).astype(BF16)
    for move in GATHER:
        ag_copy(move).wait_send()
    for off in REDUCE:
        if off not in LAST:
            rs_copy(off).wait_send()

    @pl.when(core == 0)
    def _():
        to_sibling.wait_send()

    @pl.when(core == 1)
    def _():
        total_back.wait_send()
        for copies, behind, ahead in lines:
            for i in range(most):
                @pl.when((behind >= i) & (ahead > 0))
                def _():
                    copies[i].wait_send()

    total = summed((0, 0))
    p_out[0, :, 0:BLOCK] = (total[:, 0:BLOCK] * factor_root).astype(BF16)
    p_out[0, :, BLOCK : 2 * BLOCK] = (total[:, BLOCK : 2 * BLOCK] * factor).astype(BF16)
    for off in LAST:
        rs_copy(off).wait_send()


def hand_over(*refs):
    count = (len(refs) - 1) // 2
    copies = []
    for src, dst in zip(refs[:count], refs[count:-1]):
        for at in range(0, src.shape[-2], 128):
            place = (*(0,) * (len(src.shape) - 2), pl.ds(at, 128))
            copies.append(pltpu.make_async_copy(src.at[place], dst.at[place], refs[-1].at[len(copies)]))
    for copy in copies:
        copy.start()
    for copy in copies:
        copy.wait()


def on_device(dp, queries, resp_kv, out_grad, prompt_key_value, lengths, group_mask):
    rows = queries.shape[2]
    heads = queries.shape[3] // BLOCK
    keys = CHUNKS * CHUNK
    vmem, sems = pltpu.VMEM, pltpu.SemaphoreType.DMA
    stat = vmem((heads, 8, rows), F32)
    shapes = tuple(jax.ShapeDtypeStruct(a.shape, BF16) for a in (queries, resp_kv, prompt_key_value))
    results = pl.pallas_call(
        functools.partial(kernel, dp, heads, rows, 1.0 / BLOCK**0.5),
        out_shape=tuple(pltpu.VMEM(a.shape, BF16) for a in shapes),
        in_specs=[pl.BlockSpec(memory_space=pl.ANY)] * 4 + [pl.BlockSpec(memory_space=pltpu.VMEM)] * 2,
        out_specs=[pl.BlockSpec(memory_space=pltpu.VMEM)] * 3,
        scratch_shapes=[
            vmem((rows, heads * BLOCK), BF16),
            vmem((heads * rows, BLOCK), BF16),
            vmem((rows, heads * BLOCK), BF16),
            vmem((heads * rows, BLOCK), BF16),
            vmem((heads, BLOCK, rows), BF16),
            vmem((heads, BLOCK, rows), BF16),
            vmem((keys, 2 * BLOCK), BF16),
            vmem((CHUNKS, BLOCK, CHUNK), BF16),
            vmem((CHUNKS, heads, CHUNK, rows), BF16),
            vmem((CHUNKS, heads, CHUNK, rows), F32),
            stat,
            stat,
            stat,
            vmem((CHUNKS, heads, SUBS, 8, rows), F32),
            stat,
            stat,
            stat,
            vmem((heads, BLOCK, rows), F32),
            vmem((keys, 2 * BLOCK), BF16),
            vmem((len(ORDER) - 1, BLOCK, 2 * BLOCK), BF16),
            vmem((CHUNK, BLOCK), F32),
            vmem((CHUNK, BLOCK), F32),
            vmem((dp + 2, 8, 128), F32),
            vmem((8, 128), F32),
            sems((4,)),
            sems((len(ORDER) - 1,)),
            sems((len(ORDER) - 1,)),
            sems((len(ORDER) - 1,)),
            sems((len(ORDER) - 1,)),
            sems((dp + 2,)),
            sems((dp + 2,)),
        ],
        compiler_params=pltpu.CompilerParams(
            collective_id=0, has_side_effects=True, vmem_limit_bytes=58 * 1024 * 1024
        ),
    )(queries, resp_kv, out_grad, prompt_key_value, lengths, group_mask.reshape(1, 1))
    return pl.pallas_call(
        hand_over,
        out_shape=shapes,
        in_specs=[pl.BlockSpec(memory_space=pltpu.VMEM)] * 3,
        out_specs=[pl.BlockSpec(memory_space=pl.ANY)] * 3,
        scratch_shapes=[sems((8,))],
        compiler_params=pltpu.CompilerParams(vmem_limit_bytes=1024 * 1024),
    )(*results)


def solution(mesh):
    in_specs = (
        P("dp", "group", None, None),
        P("dp", "group", None, None),
        P("dp", "group", None, None),
        P("dp", "group", None),
        P("dp", "group"),
        P("dp"),
    )
    out_specs = (P("dp", "group", None, None), P("dp", "group", None, None), P("dp", "group", None))
    return jax.shard_map(
        functools.partial(on_device, mesh.shape["dp"]), mesh=mesh, in_specs=in_specs, out_specs=out_specs, check_vma=False
    )
```
